32 devices in a mesh: freq: 8 (over z, y), tile: 4 (over x, core).
Axes of the slice: x: 2, y: 2, z: 4, core: 2. Of those that a mesh axis runs over, the one named last changes fastest.
Arguments:
- voltages: bfloat16 [1024, 262912], P(('tile', 'freq')), may hold values from -8 to 8
- gain_re: float32 [1024, 128], P(('tile', 'freq')), may hold values from -3 to 3
- gain_im: float32 [1024, 128], P(('tile', 'freq')), may hold values from -3 to 3
Outputs:
- visibility: float32 [2, 128, 1024, 1024], P(None, 'freq', 'tile')
The draws below stay inside these ranges and needn't reach their ends.
All inputs are finite; a program needn't handle non-finite values.
Results may differ from the reference program's by a relative error of at most 0.0013.
Values may be sent and summed in bfloat16 or wider, within the bound.
No kernel may reach another device: no remote copies, remote signals or barrier semaphores. Data moves between devices by JAX's collectives and lax.ppermute only.
A program may use at most 384 MiB of HBM per device.

```python
import jax
import jax.numpy as jnp
from jax import lax

INPUTS = 1024
NFFT = 256
TAPS = 4
CH = 128
FRAMES = 1024
FIRST = 0
SAMPLES = 262912


def draw_voltages(key, part):
    key = jax.random.fold_in(key, 11)
    subkeys = jax.random.split(key, 5)
    levels = jax.random.uniform(subkeys[1], (INPUTS,), jnp.float32, 0.5, 1.5)
    sources = jax.random.normal(subkeys[2], (6, SAMPLES + 64), jnp.float32)
    amplitudes = 0.6 * jax.random.normal(subkeys[3], (INPUTS, 6), jnp.float32)
    delays = jax.random.randint(subkeys[4], (INPUTS, 6), 0, 64)
    noise_key = subkeys[0]

    def one_input(operands):
        index, level, amplitude, delay = operands
        input_key = jax.random.fold_in(noise_key, index)
        receiver = jax.random.truncated_normal(input_key, -4.0, 4.0, (SAMPLES,), jnp.float32)
        signal = level * receiver
        for source in range(6):
            shifted = lax.dynamic_slice_in_dim(sources[source], delay[source], SAMPLES, 0)
            signal = signal + amplitude[source] * shifted
        return jnp.clip(signal, -8.0, 8.0).astype(jnp.bfloat16)
    indices = jnp.arange(INPUTS, dtype=jnp.int32)
    return lax.map(one_input, (indices, levels, amplitudes, delays))


def block_levels(own_key, extent, shards, low, top_value):
    gain = 1.0
    for axis_at, parts in shards:
        heights = jax.random.uniform(jax.random.fold_in(jax.random.fold_in(own_key, 6), axis_at), (parts,), jnp.float32, low / len(shards), top_value / len(shards))
        gain = gain * jnp.repeat(jnp.exp(heights), extent[axis_at] // parts).reshape((-1,) + (1,) * (len(extent) - 1 - axis_at))
    return gain


def noise(rng, dims, width, most, shards=(), kind=jnp.bfloat16):
    gain = block_levels(rng, dims, shards, -0.22, 0.18) if shards else 1.0
    array = jax.random.normal(rng, dims, jnp.float32) * width * gain
    return jnp.minimum(jnp.maximum(array, -most), most).astype(kind)


def setup_inputs(seed: int = 0) -> dict:
    seeds = jax.random.split(jax.random.key(seed), 4)
    voltages = draw_voltages(jax.random.fold_in(seeds[3], 71), 0)
    gain_re = noise(seeds[1], (INPUTS, CH), 0.7, 3.0, ((0, 32),), jnp.float32)
    gain_im = noise(seeds[2], (INPUTS, CH), 0.7, 3.0, ((0, 32),), jnp.float32)
    return dict(voltages=voltages, gain_re=gain_re, gain_im=gain_im)


def window_table():
    count = TAPS * NFFT
    sample_idx = jnp.arange(count).astype(jnp.float32)
    center = (count - 1) / 2.0
    shaped = jnp.sinc((sample_idx - center) / NFFT) * (0.5 - 0.5 * jnp.cos(2.0 * jnp.pi * sample_idx / (count - 1)))
    return shaped.reshape(TAPS, NFFT)

def fourier_table():
    sample_idx = jnp.arange(NFFT, dtype=jnp.int32)
    channel_idx = jnp.arange(CH, dtype=jnp.int32) + FIRST
    product = sample_idx[:, None] * channel_idx[None, :] % NFFT
    angle = 2.0 * jnp.pi * product.astype(jnp.float32) / NFFT
    factor = 1.0 / jnp.sqrt(jnp.float32(NFFT))
    return jnp.concatenate([jnp.cos(angle) * factor, -jnp.sin(angle) * factor], axis=1).astype(jnp.bfloat16)

def reference(voltages, gain_re, gain_im):
    window = window_table()
    fourier = fourier_table().astype(jnp.float32)
    group = min(64, INPUTS)
    count = INPUTS // group
    blocks = voltages.reshape(count, group, FRAMES + TAPS - 1, NFFT)
    gains_real = gain_re.reshape(count, group, CH)
    gains_imag = gain_im.reshape(count, group, CH)

    def analyse(operands):
        samples, weight_re, weight_im = operands
        filtered = jnp.zeros((group, FRAMES, NFFT), jnp.float32)
        for tap_index in range(TAPS):
            filtered = filtered + window[tap_index][None, None, :] * samples[:, tap_index:tap_index + FRAMES, :].astype(jnp.float32)
        filtered = filtered.astype(jnp.bfloat16)
        unscaled = jnp.einsum('ifn,nc->cif', filtered.astype(jnp.float32), fourier)
        spec_re = unscaled[:CH]
        spec_im = unscaled[CH:]
        wre = weight_re.T[:, :, None]
        wim = weight_im.T[:, :, None]
        return jnp.stack([wre * spec_re - wim * spec_im, wre * spec_im + wim * spec_re]).astype(jnp.bfloat16)
    pieces = lax.map(analyse, (blocks, gains_real, gains_imag))
    spectra = jnp.transpose(pieces, (1, 2, 0, 3, 4)).reshape(2, CH, INPUTS, FRAMES)

    def correlate(channel_data):
        values = channel_data.astype(jnp.float32)
        real_in = values[0]
        imag_in = values[1]
        real_part = jnp.dot(real_in, real_in.T, preferred_element_type=jnp.float32) + jnp.dot(imag_in, imag_in.T, preferred_element_type=jnp.float32)
        imag_part = jnp.dot(imag_in, real_in.T, preferred_element_type=jnp.float32) - jnp.dot(real_in, imag_in.T, preferred_element_type=jnp.float32)
        return jnp.stack([real_part, imag_part]) * (1.0 / FRAMES)
    result = lax.map(correlate, jnp.transpose(spectra, (1, 0, 2, 3)))
    return jnp.transpose(result, (1, 0, 2, 3))
```

```python
import functools

import jax
import jax.numpy as jnp
from jax import lax
from jax.experimental import pallas as pl
from jax.experimental.pallas import tpu as pltpu
from jax.sharding import PartitionSpec as P

NFFT = 256
TAPS = 4
CH = 128
FRAMES = 1024
FIRST = 0
LANES = 128
VMEM = 60 * 1024 * 1024


def window_table(tap_count, length):
    count = tap_count * length
    sample_idx = jnp.arange(count).astype(jnp.float32)
    center = (count - 1) / 2.0
    shaped = jnp.sinc((sample_idx - center) / length) * (
        0.5 - 0.5 * jnp.cos(2.0 * jnp.pi * sample_idx / (count - 1))
    )
    return shaped.reshape(tap_count, length)


def fourier_table(length, channels, lowest):
    sample_idx = jnp.arange(length, dtype=jnp.int32)
    channel_idx = jnp.arange(channels, dtype=jnp.int32) + lowest
    product = sample_idx[:, None] * channel_idx[None, :] % length
    angle = 2.0 * jnp.pi * product.astype(jnp.float32) / length
    factor = 1.0 / jnp.sqrt(jnp.float32(length))
    return jnp.concatenate([jnp.cos(angle) * factor, -jnp.sin(angle) * factor], axis=1).astype(
        jnp.bfloat16
    )


def chunk_sizes(channels):
    if channels == 16:
        return (2, 2, 2, 2, 2, 2, 2, 2)
    return (1,) * channels


def analyse_kernel(
    owned, freq, sizes, volt_ref, h0_ref, h1_ref, h2_ref, window_ref, table_ref, gre_ref, gim_ref, *rest
):
    outs, (low_ref, high_ref, spec_ref) = rest[: len(sizes)], rest[len(sizes) :]
    halos = (h0_ref, h1_ref, h2_ref)

    def tap(position):
        if isinstance(position, int) and position >= LANES:
            return halos[position - LANES][...].astype(jnp.float32)
        return volt_ref[:, pl.ds(pl.multiple_of(position * NFFT, NFFT), NFFT)].astype(jnp.float32)

    def filter_at(position, store):
        total = window_ref[0:1, :] * tap(position)
        for p in range(1, TAPS):
            total = total + window_ref[p : p + 1, :] * tap(position + p)
        at = pl.ds(pl.multiple_of(store * owned, owned), owned)
        low_ref[at, :] = total[:, :LANES]
        high_ref[at, :] = total[:, LANES:]

    group = 4

    def step(g, carry):
        base = g * group
        for u in range(group):
            filter_at(base + u, base + u)
        return carry

    lax.fori_loop(0, LANES // group - 1, step, 0)
    for position in range(LANES - group, LANES):
        filter_at(position, position)

    pair = 2

    def transform(g, carry):
        rows = jnp.concatenate(
            [
                jnp.concatenate(
                    [ref[pl.ds(g * pair + u, LANES, stride=owned), :] for ref in (low_ref, high_ref)],
                    axis=1,
                )
                for u in range(pair)
            ],
            axis=0,
        ).astype(jnp.bfloat16)
        result = lax.dot_general(
            table_ref[...], rows, (((1,), (1,)), ((), ())), preferred_element_type=jnp.float32
        )
        for u in range(pair):
            spec_ref[pl.ds(g * pair + u, 2 * CH, stride=owned), :] = result[
                :, u * LANES : (u + 1) * LANES
            ]
        return carry

    lax.fori_loop(0, owned // pair, transform, 0)

    channels = CH // freq
    start = 0
    for k, size in enumerate(sizes):
        for u in range(size):

            def finish(dest, carry, k=k, u=u, place=start + u):
                channel = dest * channels + place
                at = pl.ds(pl.multiple_of(channel * owned, owned), owned)
                im_at = pl.ds(pl.multiple_of((CH + channel) * owned, owned), owned)
                re, im = spec_ref[at, :], spec_ref[im_at, :]
                gre, gim = gre_ref[at, :], gim_ref[at, :]
                outs[k][dest, u, 0] = (gre * re - gim * im).astype(jnp.bfloat16)
                outs[k][dest, u, 1] = (gre * im + gim * re).astype(jnp.bfloat16)
                return carry

            lax.fori_loop(0, freq, finish, 0, unroll=min(freq, 8))
        start += size


def analyse(voltages, gain_re, gain_im, freq, sizes):
    owned = voltages.shape[0]
    span = LANES * NFFT
    table = fourier_table(NFFT, CH, FIRST).T
    window = window_table(TAPS, NFFT)

    def spread(gain):
        return jnp.broadcast_to(gain.T[:, :, None], (CH, owned, LANES)).reshape(CH * owned, LANES)

    halo = [
        pl.BlockSpec((owned, NFFT), lambda b, q=q: (0, (b + 1) * LANES + q)) for q in range(TAPS - 1)
    ]
    whole = lambda shape: pl.BlockSpec(shape, lambda b: (0, 0))
    return pl.pallas_call(
        functools.partial(analyse_kernel, owned, freq, sizes),
        grid=(FRAMES // LANES,),
        in_specs=[
            pl.BlockSpec((owned, span), lambda b: (0, b)),
            *halo,
            whole((TAPS, NFFT)),
            whole((2 * CH, NFFT)),
            whole((CH * owned, LANES)),
            whole((CH * owned, LANES)),
        ],
        out_specs=[
            pl.BlockSpec((freq, size, 2, owned, LANES), lambda b: (0, 0, 0, 0, b)) for size in sizes
        ],
        out_shape=[
            jax.ShapeDtypeStruct((freq, size, 2, owned, FRAMES), jnp.bfloat16) for size in sizes
        ],
        scratch_shapes=[
            pltpu.VMEM((LANES * owned, LANES), jnp.float32),
            pltpu.VMEM((LANES * owned, LANES), jnp.float32),
            pltpu.VMEM((2 * CH * owned, LANES), jnp.float32),
        ],
        compiler_params=pltpu.CompilerParams(vmem_limit_bytes=VMEM),
        cost_estimate=pl.CostEstimate(
            flops=2 * owned * FRAMES * NFFT * 2 * CH, bytes_accessed=4 * voltages.size, transcendentals=0
        ),
    )(voltages, voltages, voltages, voltages, window, table, spread(gain_re), spread(gain_im))


def correlate_kernel(tiles, me_ref, *rest):
    blocks, out_ref, left_ref = rest[:tiles], rest[-2], rest[-1]
    own = blocks[0]
    rows = own.shape[0] * own.shape[3]
    re = own[:, 0, 0].reshape(rows, FRAMES)
    im = own[:, 0, 1].reshape(rows, FRAMES)
    left_ref[0:rows, 0:FRAMES] = re
    left_ref[0:rows, FRAMES:] = im
    left_ref[rows:, 0:FRAMES] = im
    left_ref[rows:, FRAMES:] = -re
    factor = 1.0 / FRAMES
    for r in range(tiles):
        other = jnp.concatenate(
            [blocks[r][:, 0, 0].reshape(rows, FRAMES), blocks[r][:, 0, 1].reshape(rows, FRAMES)], axis=1
        )
        both = lax.dot_general(
            left_ref[...], other, (((1,), (1,)), ((), ())), preferred_element_type=jnp.float32
        )
        at = pl.ds(pl.multiple_of((me_ref[0] ^ r) * rows, rows), rows)
        out_ref[0, 0, :, at] = both[:rows] * factor
        out_ref[1, 0, :, at] = both[rows:] * factor


def correlate(me, blocks, previous, first, channels):
    freq, size, _, owned, frames = blocks[0].shape
    tiles = len(blocks)
    rows = freq * owned
    in_specs = [
        pl.BlockSpec((freq, 1, 2, owned, frames), lambda c, me: (0, c, 0, 0, 0)) for _ in blocks
    ]
    args = [me, *blocks]
    aliases = {}
    if previous is not None:
        in_specs.append(pl.BlockSpec(memory_space=pl.ANY))
        aliases = {len(args): 0}
        args.append(previous)
    return pl.pallas_call(
        functools.partial(correlate_kernel, tiles),
        grid_spec=pltpu.PrefetchScalarGridSpec(
            num_scalar_prefetch=1,
            grid=(size,),
            in_specs=in_specs,
            out_specs=pl.BlockSpec((2, 1, rows, tiles * rows), lambda c, me: (0, first + c, 0, 0)),
            scratch_shapes=[pltpu.VMEM((2 * rows, 2 * frames), jnp.bfloat16)],
        ),
        out_shape=jax.ShapeDtypeStruct((2, channels, rows, tiles * rows), jnp.float32),
        input_output_aliases=aliases,
        compiler_params=pltpu.CompilerParams(vmem_limit_bytes=VMEM),
        cost_estimate=pl.CostEstimate(
            flops=size * 2 * (2 * rows) * (2 * frames) * (tiles * rows),
            bytes_accessed=size * (tiles * rows * frames * 4 + 2 * rows * tiles * rows * 4),
            transcendentals=0,
        ),
    )(*args)


def per_device(freq, tile, voltages, gain_re, gain_im):
    channels = CH // freq
    sizes = chunk_sizes(channels)
    me = lax.axis_index("tile").astype(jnp.int32).reshape(1)
    messages = list(analyse(voltages, gain_re, gain_im, freq, sizes))

    def swap(array, bit):
        return lax.ppermute(array, "tile", [(t, t ^ bit) for t in range(tile)])

    count = len(sizes)
    firsts = [sum(sizes[:k]) for k in range(count)]
    turned, across, beside, opposite = ([None] * count for _ in range(4))
    result = None

    def finish(k):
        blocks = [turned[k], beside[k], across[k], opposite[k]]
        return correlate(me, blocks, result, firsts[k], channels)

    for k in range(count):
        message = messages[k]
        if k >= 2:
            message, across[k - 2] = lax.optimization_barrier((message, across[k - 2]))
            opposite[k - 2] = swap(across[k - 2], 1)
        if k >= 3:
            message, opposite[k - 3], beside[k - 3] = lax.optimization_barrier(
                (message, opposite[k - 3], beside[k - 3])
            )
            if k >= 4:
                message, result = lax.optimization_barrier((message, result))
            result = finish(k - 3)
        turned[k] = lax.all_to_all(message, "freq", split_axis=0, concat_axis=0, tiled=True)
        across[k] = swap(turned[k], 2)
        beside[k] = swap(turned[k], 1)
    for k in range(count - 2, count):
        opposite[k] = swap(across[k], 1)
    for k in range(count - 3, count):
        result = finish(k)
    return result


def solution(mesh):
    in_specs = (P(("tile", "freq"), None), P(("tile", "freq"), None), P(("tile", "freq"), None))
    out_specs = P(None, "freq", "tile", None)
    return jax.shard_map(
        functools.partial(per_device, mesh.shape["freq"], mesh.shape["tile"]),
        mesh=mesh,
        in_specs=in_specs,
        out_specs=out_specs,
        check_vma=False,
    )
```

```python
import functools

import jax
import jax.numpy as jnp
from jax import lax
from jax.experimental import pallas as pl
from jax.experimental.pallas import tpu as pltpu
from jax.sharding import PartitionSpec as P

NFFT = 256
TAPS = 4
CH = 128
FRAMES = 1024
FIRST = 0
LANES = 128
VMEM = 60 * 1024 * 1024


def window_table(tap_count, length):
    count = tap_count * length
    sample_idx = jnp.arange(count).astype(jnp.float32)
    center = (count - 1) / 2.0
    shaped = jnp.sinc((sample_idx - center) / length) * (
        0.5 - 0.5 * jnp.cos(2.0 * jnp.pi * sample_idx / (count - 1))
    )
    return shaped.reshape(tap_count, length)


def fourier_table(length, channels, lowest, freq):
    owned = channels // freq
    row = jnp.arange(2 * channels, dtype=jnp.int32)
    place, part, dest = row // (2 * freq), row // freq % 2, row % freq
    channel_idx = dest * owned + place + lowest
    sample_idx = jnp.arange(length, dtype=jnp.int32)
    product = sample_idx[None, :] * channel_idx[:, None] % length
    angle = 2.0 * jnp.pi * product.astype(jnp.float32) / length
    factor = 1.0 / jnp.sqrt(jnp.float32(length))
    return jnp.where(part[:, None] == 0, jnp.cos(angle) * factor, -jnp.sin(angle) * factor).astype(
        jnp.bfloat16
    )


def chunk_sizes(channels):
    if channels == 16:
        return (2, 2, 2, 2, 2, 2, 2, 2)
    return (1,) * channels


def analyse_kernel(
    owned, freq, low, sizes, volt_ref, h0_ref, h1_ref, h2_ref, window_ref, table_ref, gre_ref, gim_ref, *rest
):
    outs, (low_ref, high_ref, spec_ref, wre_ref, wim_ref) = rest[: len(sizes)], rest[len(sizes) :]
    halos = (h0_ref, h1_ref, h2_ref)

    @pl.when(pl.program_id(0) == 0)
    def _():
        for source, spread in ((gre_ref, wre_ref), (gim_ref, wim_ref)):
            gain = source[...]
            for c in range(CH):
                spread[c * owned : (c + 1) * owned, :] = jnp.broadcast_to(
                    gain[:, c : c + 1], (owned, LANES)
                )

    group = 8
    last = LANES // group - 1
    for half, ref in enumerate((low_ref, high_ref)):
        lanes = slice(half * LANES, (half + 1) * LANES)
        weights = [
            jnp.broadcast_to(window_ref[p : p + 1, lanes], (owned, LANES)) for p in range(TAPS)
        ]

        def load(position, half=half):
            at = pl.ds(pl.multiple_of(position * NFFT + half * LANES, LANES), LANES)
            return volt_ref[:, at].astype(jnp.float32)

        def emit(position, taps, weights=weights, ref=ref):
            total = weights[0] * taps[0]
            for p in range(1, TAPS):
                total = total + weights[p] * taps[p]
            ref[pl.ds(pl.multiple_of(position * owned, owned), owned), :] = total

        def step(g, carry, load=load, emit=emit):
            taps = list(carry)
            for u in range(group):
                taps.append(load(g * group + u + TAPS - 1))
                emit(g * group + u, taps[-TAPS:])
            return tuple(taps[1 - TAPS :])

        taps = list(lax.fori_loop(0, last, step, tuple(load(p) for p in range(TAPS - 1))))
        for position in range(last * group, LANES):
            ahead = position + TAPS - 1
            if ahead < LANES:
                taps.append(load(ahead))
            else:
                taps.append(halos[ahead - LANES][:, lanes].astype(jnp.float32))
            emit(position, taps[-TAPS:])

    pair = 2
    rows_of = lambda place: 2 * freq * place
    count = rows_of(sum(sizes))
    table = table_ref[rows_of(low) : rows_of(low) + count, :]
    for g in range(owned // pair):
        rows = jnp.concatenate(
            [
                jnp.concatenate(
                    [ref[pl.ds(g * pair + u, LANES, stride=owned), :] for ref in (low_ref, high_ref)],
                    axis=1,
                )
                for u in range(pair)
            ],
            axis=0,
        ).astype(jnp.bfloat16)
        result = lax.dot_general(
            table, rows, (((1,), (1,)), ((), ())), preferred_element_type=jnp.float32
        )
        for u in range(pair):
            spec_ref[pl.ds(g * pair + u, count, stride=owned), :] = result[
                :, u * LANES : (u + 1) * LANES
            ]

    channels = CH // freq
    start = 0
    for k, size in enumerate(sizes):
        for u in range(size):
            for dest in range(freq):
                row = (rows_of(start + u) + dest) * owned
                re = spec_ref[row : row + owned, :]
                im = spec_ref[row + freq * owned : row + (freq + 1) * owned, :]
                at = (dest * channels + low + start + u) * owned
                wre, wim = wre_ref[at : at + owned, :], wim_ref[at : at + owned, :]
                outs[k][dest, u, 0] = (wre * re - wim * im).astype(jnp.bfloat16)
                outs[k][dest, u, 1] = (wre * im + wim * re).astype(jnp.bfloat16)
        start += size


def analyse(voltages, window, table, gain_re, gain_im, freq, low, sizes, first, count):
    owned = voltages.shape[0]
    halo = [
        pl.BlockSpec((owned, NFFT), lambda b, q=q: (0, (first + b + 1) * LANES + q))
        for q in range(TAPS - 1)
    ]
    whole = lambda shape: pl.BlockSpec(shape, lambda b: (0, 0))
    return pl.pallas_call(
        functools.partial(analyse_kernel, owned, freq, low, sizes),
        grid=(count,),
        in_specs=[
            pl.BlockSpec((owned, LANES * NFFT), lambda b: (0, first + b)),
            *halo,
            whole((TAPS, NFFT)),
            whole((2 * CH, NFFT)),
            whole((owned, CH)),
            whole((owned, CH)),
        ],
        out_specs=[
            pl.BlockSpec((freq, size, 2, owned, LANES), lambda b: (0, 0, 0, 0, b)) for size in sizes
        ],
        out_shape=[
            jax.ShapeDtypeStruct((freq, size, 2, owned, count * LANES), jnp.bfloat16)
            for size in sizes
        ],
        scratch_shapes=[
            pltpu.VMEM((LANES * owned, LANES), jnp.float32),
            pltpu.VMEM((LANES * owned, LANES), jnp.float32),
            pltpu.VMEM((2 * freq * sum(sizes) * owned, LANES), jnp.float32),
            pltpu.VMEM((CH * owned, LANES), jnp.float32),
            pltpu.VMEM((CH * owned, LANES), jnp.float32),
        ],
        compiler_params=pltpu.CompilerParams(vmem_limit_bytes=VMEM),
        cost_estimate=pl.CostEstimate(
            flops=2 * owned * count * LANES * NFFT * 2 * CH * 8,
            bytes_accessed=4 * owned * count * LANES * NFFT,
            transcendentals=0,
        ),
    )(voltages, voltages, voltages, voltages, window, table, gain_re, gain_im)


def correlate_kernel(tiles, me_ref, *rest):
    heads, bodies, out_ref, left_ref = rest[:tiles], rest[tiles : 2 * tiles], rest[-2], rest[-1]
    rows = heads[0].shape[0] * heads[0].shape[3]

    def part(r, p):
        return [ref[r][:, 0, p].reshape(rows, -1) for ref in (heads, bodies)]

    re = jnp.concatenate(part(0, 0), axis=1)
    im = jnp.concatenate(part(0, 1), axis=1)
    left_ref[0:rows, 0:FRAMES] = re
    left_ref[0:rows, FRAMES:] = im
    left_ref[rows:, 0:FRAMES] = im
    left_ref[rows:, FRAMES:] = -re
    factor = 1.0 / FRAMES
    for r in range(tiles):
        other = jnp.concatenate([*part(r, 0), *part(r, 1)], axis=1)
        both = lax.dot_general(
            left_ref[...], other, (((1,), (1,)), ((), ())), preferred_element_type=jnp.float32
        )
        at = pl.ds(pl.multiple_of((me_ref[0] ^ r) * rows, rows), rows)
        out_ref[0, 0, :, at] = both[:rows] * factor
        out_ref[1, 0, :, at] = both[rows:] * factor


def correlate(me, heads, bodies, previous, first, channels):
    freq, size, _, owned, _ = bodies[0].shape
    tiles = len(bodies)
    rows = freq * owned
    in_specs = [
        pl.BlockSpec((freq, 1, 2, owned, x.shape[-1]), lambda c, me: (0, first + c, 0, 0, 0))
        for x in heads
    ] + [
        pl.BlockSpec((freq, 1, 2, owned, x.shape[-1]), lambda c, me: (0, c, 0, 0, 0)) for x in bodies
    ]
    args = [me, *heads, *bodies]
    aliases = {}
    if previous is not None:
        in_specs.append(pl.BlockSpec(memory_space=pl.ANY))
        aliases = {len(args): 0}
        args.append(previous)
    return pl.pallas_call(
        functools.partial(correlate_kernel, tiles),
        grid_spec=pltpu.PrefetchScalarGridSpec(
            num_scalar_prefetch=1,
            grid=(size,),
            in_specs=in_specs,
            out_specs=pl.BlockSpec((2, 1, rows, tiles * rows), lambda c, me: (0, first + c, 0, 0)),
            scratch_shapes=[pltpu.VMEM((2 * rows, 2 * FRAMES), jnp.bfloat16)],
        ),
        out_shape=jax.ShapeDtypeStruct((2, channels, rows, tiles * rows), jnp.float32),
        input_output_aliases=aliases,
        compiler_params=pltpu.CompilerParams(vmem_limit_bytes=VMEM),
        cost_estimate=pl.CostEstimate(
            flops=size * 2 * (2 * rows) * (2 * FRAMES) * (tiles * rows),
            bytes_accessed=size * (tiles * rows * FRAMES * 4 + 2 * rows * tiles * rows * 4),
            transcendentals=0,
        ),
    )(*args)


def per_device(freq, tile, voltages, gain_re, gain_im):
    channels = CH // freq
    sizes = chunk_sizes(channels)
    me = lax.axis_index("tile").astype(jnp.int32).reshape(1)
    tables = (
        window_table(TAPS, NFFT),
        fourier_table(NFFT, CH, FIRST, freq),
        gain_re,
        gain_im,
    )
    blocks = FRAMES // LANES
    messages = list(analyse(voltages, *tables, freq, 0, (channels,), 0, 1))
    lead = len(sizes) // 4
    messages += analyse(voltages, *tables, freq, 0, sizes[:lead], 1, blocks - 1)
    messages[1], again = lax.optimization_barrier((messages[1], voltages))
    messages += analyse(again, *tables, freq, sum(sizes[:lead]), sizes[lead:], 1, blocks - 1)

    def swap(array, bit):
        return lax.ppermute(array, "tile", [(t, t ^ bit) for t in range(tile)])

    count = len(messages)
    firsts = [sum(sizes[:k]) for k in range(count)]
    turned, across, beside, opposite, results = ([None] * count for _ in range(5))

    def finish(k):
        heads, bodies = (
            [turned[m], beside[m], across[m], opposite[m]] for m in (0, k)
        )
        results[k] = correlate(me, heads, bodies, results[k - 1], firsts[k - 1], channels)

    def after(array, *waits):
        waits = [w for w in waits if w is not None]
        return lax.optimization_barrier((array, *waits))[0] if waits else array

    lag = 2
    for k in range(count):
        message = messages[k]
        if k >= lag:
            message = after(message, across[k - lag], beside[k - lag])
        if k >= lag + 1:
            message = after(message, opposite[k - lag - 1])
        if k >= lag + 2:
            message = after(message, results[k - lag - 2])
        turned[k] = lax.all_to_all(message, "freq", split_axis=0, concat_axis=0, tiled=True)
        across[k] = swap(turned[k], 2)
        beside[k] = swap(turned[k], 1)
        source = across[k]
        if k == count - 1:
            source = after(source, results[k - 1])
        opposite[k] = swap(source, 1)
        if k >= 1:
            finish(k)
    return results[-1]


def solution(mesh):
    in_specs = (P(("tile", "freq"), None), P(("tile", "freq"), None), P(("tile", "freq"), None))
    out_specs = P(None, "freq", "tile", None)
    return jax.shard_map(
        functools.partial(per_device, mesh.shape["freq"], mesh.shape["tile"]),
        mesh=mesh,
        in_specs=in_specs,
        out_specs=out_specs,
        check_vma=False,
    )
```

```python
import functools

import jax
import jax.numpy as jnp
from jax import lax
from jax.experimental import pallas as pl
from jax.experimental.pallas import tpu as pltpu
from jax.sharding import PartitionSpec as P

NFFT = 256
TAPS = 4
CH = 128
FRAMES = 1024
FIRST = 0
LANES = 128
VMEM = 60 * 1024 * 1024


def window_table(tap_count, length):
    count = tap_count * length
    sample_idx = jnp.arange(count).astype(jnp.float32)
    center = (count - 1) / 2.0
    shaped = jnp.sinc((sample_idx - center) / length) * (
        0.5 - 0.5 * jnp.cos(2.0 * jnp.pi * sample_idx / (count - 1))
    )
    return shaped.reshape(tap_count, length)


def fourier_table(length, channels, lowest, freq):
    owned = channels // freq
    row = jnp.arange(2 * channels, dtype=jnp.int32)
    place, part, dest = row // (2 * freq), row // freq % 2, row % freq
    channel_idx = dest * owned + place + lowest
    sample_idx = jnp.arange(length, dtype=jnp.int32)
    product = sample_idx[None, :] * channel_idx[:, None] % length
    angle = 2.0 * jnp.pi * product.astype(jnp.float32) / length
    factor = 1.0 / jnp.sqrt(jnp.float32(length))
    return jnp.where(part[:, None] == 0, jnp.cos(angle) * factor, -jnp.sin(angle) * factor).astype(
        jnp.bfloat16
    )


def chunk_sizes(channels):
    if channels == 16:
        return (2, 2, 2, 2, 2, 2, 2, 2)
    return (1,) * channels


def analyse_kernel(
    owned, freq, low, sizes, volt_ref, h0_ref, h1_ref, h2_ref, window_ref, table_ref, gre_ref, gim_ref, *rest
):
    outs, (low_ref, high_ref, spec_ref, wre_ref, wim_ref) = rest[: len(sizes)], rest[len(sizes) :]
    halos = (h0_ref, h1_ref, h2_ref)

    @pl.when(pl.program_id(0) == 0)
    def _():
        for source, spread in ((gre_ref, wre_ref), (gim_ref, wim_ref)):
            gain = source[...]
            for c in range(CH):
                spread[c * owned : (c + 1) * owned, :] = jnp.broadcast_to(
                    gain[:, c : c + 1], (owned, LANES)
                )

    group = 8
    last = LANES // group - 1
    for half, ref in enumerate((low_ref, high_ref)):
        lanes = slice(half * LANES, (half + 1) * LANES)
        weights = [
            jnp.broadcast_to(window_ref[p : p + 1, lanes], (owned, LANES)) for p in range(TAPS)
        ]

        def load(position, half=half):
            at = pl.ds(pl.multiple_of(position * NFFT + half * LANES, LANES), LANES)
            return volt_ref[:, at].astype(jnp.float32)

        def emit(position, taps, weights=weights, ref=ref):
            total = weights[0] * taps[0]
            for p in range(1, TAPS):
                total = total + weights[p] * taps[p]
            ref[pl.ds(pl.multiple_of(position * owned, owned), owned), :] = total

        def step(g, carry, load=load, emit=emit):
            taps = list(carry)
            for u in range(group):
                taps.append(load(g * group + u + TAPS - 1))
                emit(g * group + u, taps[-TAPS:])
            return tuple(taps[1 - TAPS :])

        taps = list(lax.fori_loop(0, last, step, tuple(load(p) for p in range(TAPS - 1))))
        for position in range(last * group, LANES):
            ahead = position + TAPS - 1
            if ahead < LANES:
                taps.append(load(ahead))
            else:
                taps.append(halos[ahead - LANES][:, lanes].astype(jnp.float32))
            emit(position, taps[-TAPS:])

    pair = 2
    rows_of = lambda place: 2 * freq * place
    count = rows_of(sum(sizes))
    table = table_ref[rows_of(low) : rows_of(low) + count, :]
    for g in range(owned // pair):
        rows = jnp.concatenate(
            [
                jnp.concatenate(
                    [ref[pl.ds(g * pair + u, LANES, stride=owned), :] for ref in (low_ref, high_ref)],
                    axis=1,
                )
                for u in range(pair)
            ],
            axis=0,
        ).astype(jnp.bfloat16)
        result = lax.dot_general(
            table, rows, (((1,), (1,)), ((), ())), preferred_element_type=jnp.float32
        )
        for u in range(pair):
            spec_ref[pl.ds(g * pair + u, count, stride=owned), :] = result[
                :, u * LANES : (u + 1) * LANES
            ]

    channels = CH // freq
    start = 0
    for k, size in enumerate(sizes):
        for u in range(size):
            for dest in range(freq):
                row = (rows_of(start + u) + dest) * owned
                re = spec_ref[row : row + owned, :]
                im = spec_ref[row + freq * owned : row + (freq + 1) * owned, :]
                at = (dest * channels + low + start + u) * owned
                wre, wim = wre_ref[at : at + owned, :], wim_ref[at : at + owned, :]
                outs[k][dest, u, 0] = (wre * re - wim * im).astype(jnp.bfloat16)
                outs[k][dest, u, 1] = (wre * im + wim * re).astype(jnp.bfloat16)
        start += size


def analyse(voltages, window, table, gain_re, gain_im, freq, low, sizes, first, count):
    owned = voltages.shape[0]
    halo = [
        pl.BlockSpec((owned, NFFT), lambda b, q=q: (0, (first + b + 1) * LANES + q))
        for q in range(TAPS - 1)
    ]
    whole = lambda shape: pl.BlockSpec(shape, lambda b: (0, 0))
    return pl.pallas_call(
        functools.partial(analyse_kernel, owned, freq, low, sizes),
        grid=(count,),
        in_specs=[
            pl.BlockSpec((owned, LANES * NFFT), lambda b: (0, first + b)),
            *halo,
            whole((TAPS, NFFT)),
            whole((2 * CH, NFFT)),
            whole((owned, CH)),
            whole((owned, CH)),
        ],
        out_specs=[
            pl.BlockSpec((freq, size, 2, owned, LANES), lambda b: (0, 0, 0, 0, b)) for size in sizes
        ],
        out_shape=[
            jax.ShapeDtypeStruct((freq, size, 2, owned, count * LANES), jnp.bfloat16)
            for size in sizes
        ],
        scratch_shapes=[
            pltpu.VMEM((LANES * owned, LANES), jnp.float32),
            pltpu.VMEM((LANES * owned, LANES), jnp.float32),
            pltpu.VMEM((2 * freq * sum(sizes) * owned, LANES), jnp.float32),
            pltpu.VMEM((CH * owned, LANES), jnp.float32),
            pltpu.VMEM((CH * owned, LANES), jnp.float32),
        ],
        compiler_params=pltpu.CompilerParams(vmem_limit_bytes=VMEM),
        cost_estimate=pl.CostEstimate(
            flops=2 * owned * count * LANES * NFFT * 2 * CH * 8,
            bytes_accessed=4 * owned * count * LANES * NFFT,
            transcendentals=0,
        ),
    )(voltages, voltages, voltages, voltages, window, table, gain_re, gain_im)


def correlate_kernel(steps, me_ref, *rest):
    count = len(steps) + (0 not in steps)
    heads, bodies, out_ref, left_ref = rest[:count], rest[count : 2 * count], rest[-2], rest[-1]
    rows = heads[0].shape[0] * heads[0].shape[3]

    def part(r, p):
        return [ref[r][:, 0, p].reshape(rows, -1) for ref in (heads, bodies)]

    re = jnp.concatenate(part(0, 0), axis=1)
    im = jnp.concatenate(part(0, 1), axis=1)
    left_ref[0:rows, 0:FRAMES] = re
    left_ref[0:rows, FRAMES:] = im
    left_ref[rows:, 0:FRAMES] = im
    left_ref[rows:, FRAMES:] = -re
    factor = 1.0 / FRAMES
    for place, step in enumerate(steps):
        r = count - len(steps) + place
        other = jnp.concatenate([*part(r, 0), *part(r, 1)], axis=1)
        both = lax.dot_general(
            left_ref[...], other, (((1,), (1,)), ((), ())), preferred_element_type=jnp.float32
        )
        column = (me_ref[0] ^ step) % len(steps)
        at = pl.ds(pl.multiple_of(column * rows, rows), rows)
        out_ref[0, 0, :, at] = both[:rows] * factor
        out_ref[1, 0, :, at] = both[rows:] * factor


def correlate(me, tiles, steps, heads, bodies, previous, first, channels):
    freq, size, _, owned, _ = bodies[0].shape
    rows = freq * owned
    width = len(steps)
    in_specs = [
        pl.BlockSpec((freq, 1, 2, owned, x.shape[-1]), lambda c, me: (0, first + c, 0, 0, 0))
        for x in heads
    ] + [
        pl.BlockSpec((freq, 1, 2, owned, x.shape[-1]), lambda c, me: (0, c, 0, 0, 0)) for x in bodies
    ]
    args = [me, *heads, *bodies]
    aliases = {}
    if previous is not None:
        in_specs.append(pl.BlockSpec(memory_space=pl.ANY))
        aliases = {len(args): 0}
        args.append(previous)
    return pl.pallas_call(
        functools.partial(correlate_kernel, steps),
        grid_spec=pltpu.PrefetchScalarGridSpec(
            num_scalar_prefetch=1,
            grid=(size,),
            in_specs=in_specs,
            out_specs=pl.BlockSpec(
                (2, 1, rows, width * rows),
                lambda c, me: (0, first + c, 0, (me[0] ^ steps[0]) // width),
            ),
            scratch_shapes=[pltpu.VMEM((2 * rows, 2 * FRAMES), jnp.bfloat16)],
        ),
        out_shape=jax.ShapeDtypeStruct((2, channels, rows, tiles * rows), jnp.float32),
        input_output_aliases=aliases,
        compiler_params=pltpu.CompilerParams(vmem_limit_bytes=VMEM),
        cost_estimate=pl.CostEstimate(
            flops=size * 2 * (2 * rows) * (2 * FRAMES) * (width * rows),
            bytes_accessed=size * (tiles * rows * FRAMES * 4 + 2 * rows * width * rows * 4),
            transcendentals=0,
        ),
    )(*args)


def per_device(freq, tile, voltages, gain_re, gain_im):
    channels = CH // freq
    sizes = chunk_sizes(channels)
    me = lax.axis_index("tile").astype(jnp.int32).reshape(1)
    tables = (
        window_table(TAPS, NFFT),
        fourier_table(NFFT, CH, FIRST, freq),
        gain_re,
        gain_im,
    )
    blocks = FRAMES // LANES
    messages = list(analyse(voltages, *tables, freq, 0, (channels,), 0, 1))
    lead = len(sizes) // 4
    messages += analyse(voltages, *tables, freq, 0, sizes[:lead], 1, blocks - 1)
    messages[1], again = lax.optimization_barrier((messages[1], voltages))
    messages += analyse(again, *tables, freq, sum(sizes[:lead]), sizes[lead:], 1, blocks - 1)
    if lead > 1:
        messages[lead], messages[lead + 1] = lax.optimization_barrier(
            (messages[lead], messages[lead + 1])
        )

    def swap(array, bit):
        return lax.ppermute(array, "tile", [(t, t ^ bit) for t in range(tile)])

    count = len(messages)
    firsts = [sum(sizes[:k]) for k in range(count)]
    turned, across, beside, opposite, results = ([None] * count for _ in range(5))

    def finish(k, steps):
        parts = (turned, beside, across, opposite)
        wanted = steps if 0 in steps else (0, *steps)
        heads, bodies = ([parts[step][m] for step in wanted] for m in (0, k))
        before = results[k] if results[k] is not None else results[k - 1]
        results[k] = correlate(me, tile, steps, heads, bodies, before, firsts[k - 1], channels)

    def after(array, *waits):
        waits = [w for w in waits if w is not None]
        return lax.optimization_barrier((array, *waits))[0] if waits else array

    lag = 2
    for k in range(count):
        message = messages[k]
        if k >= lag:
            message = after(message, across[k - lag], beside[k - lag])
        if k >= lag + 1:
            message = after(message, opposite[k - lag - 1])
        if k >= lag + 2:
            message = after(message, results[k - lag - 2])
        turned[k] = lax.all_to_all(message, "freq", split_axis=0, concat_axis=0, tiled=True)
        across[k] = swap(turned[k], 2)
        beside[k] = swap(turned[k], 1)
        source = across[k]
        if k == count - 1:
            finish(k, (0, 1))
            source = after(source, results[k])
        opposite[k] = swap(source, 1)
        if k >= 1:
            finish(k, (2, 3) if k == count - 1 else (0, 1, 2, 3))
    return results[-1]


def solution(mesh):
    in_specs = (P(("tile", "freq"), None), P(("tile", "freq"), None), P(("tile", "freq"), None))
    out_specs = P(None, "freq", "tile", None)
    return jax.shard_map(
        functools.partial(per_device, mesh.shape["freq"], mesh.shape["tile"]),
        mesh=mesh,
        in_specs=in_specs,
        out_specs=out_specs,
        check_vma=False,
    )
```

```python
import functools

import jax
import jax.numpy as jnp
from jax import lax
from jax.experimental import pallas as pl
from jax.experimental.pallas import tpu as pltpu
from jax.sharding import PartitionSpec as P

NFFT = 256
TAPS = 4
CH = 128
FRAMES = 1024
FIRST = 0
LANES = 128
VMEM = 60 * 1024 * 1024


def window_table(tap_count, length):
    count = tap_count * length
    sample_idx = jnp.arange(count).astype(jnp.float32)
    center = (count - 1) / 2.0
    shaped = jnp.sinc((sample_idx - center) / length) * (
        0.5 - 0.5 * jnp.cos(2.0 * jnp.pi * sample_idx / (count - 1))
    )
    return shaped.reshape(tap_count, length)


def fourier_table(length, channels, lowest, freq):
    owned = channels // freq
    row = jnp.arange(2 * channels, dtype=jnp.int32)
    place, part, dest = row // (2 * freq), row // freq % 2, row % freq
    channel_idx = dest * owned + place + lowest
    sample_idx = jnp.arange(length, dtype=jnp.int32)
    product = sample_idx[None, :] * channel_idx[:, None] % length
    angle = 2.0 * jnp.pi * product.astype(jnp.float32) / length
    factor = 1.0 / jnp.sqrt(jnp.float32(length))
    return jnp.where(part[:, None] == 0, jnp.cos(angle) * factor, -jnp.sin(angle) * factor).astype(
        jnp.bfloat16
    )


def chunk_sizes(channels):
    if channels == 16:
        return (2, 2, 2, 2, 2, 2, 2, 1, 1)
    return (1,) * channels


def analyse_kernel(
    owned, freq, low, sizes, volt_ref, h0_ref, h1_ref, h2_ref, window_ref, table_ref, gre_ref, gim_ref, *rest
):
    outs, (low_ref, high_ref, spec_ref, wre_ref, wim_ref) = rest[: len(sizes)], rest[len(sizes) :]
    halos = (h0_ref, h1_ref, h2_ref)

    @pl.when(pl.program_id(0) == 0)
    def _():
        for source, spread in ((gre_ref, wre_ref), (gim_ref, wim_ref)):
            gain = source[...]
            for c in range(CH):
                spread[c * owned : (c + 1) * owned, :] = jnp.broadcast_to(
                    gain[:, c : c + 1], (owned, LANES)
                )

    group = 8
    last = LANES // group - 1
    for half, ref in enumerate((low_ref, high_ref)):
        lanes = slice(half * LANES, (half + 1) * LANES)
        weights = [
            jnp.broadcast_to(window_ref[p : p + 1, lanes], (owned, LANES)) for p in range(TAPS)
        ]

        def load(position, half=half):
            at = pl.ds(pl.multiple_of(position * NFFT + half * LANES, LANES), LANES)
            return volt_ref[:, at].astype(jnp.float32)

        def emit(position, taps, weights=weights, ref=ref):
            total = weights[0] * taps[0]
            for p in range(1, TAPS):
                total = total + weights[p] * taps[p]
            ref[pl.ds(pl.multiple_of(position * owned, owned), owned), :] = total

        def step(g, carry, load=load, emit=emit):
            taps = list(carry)
            for u in range(group):
                taps.append(load(g * group + u + TAPS - 1))
                emit(g * group + u, taps[-TAPS:])
            return tuple(taps[1 - TAPS :])

        taps = list(lax.fori_loop(0, last, step, tuple(load(p) for p in range(TAPS - 1))))
        for position in range(last * group, LANES):
            ahead = position + TAPS - 1
            if ahead < LANES:
                taps.append(load(ahead))
            else:
                taps.append(halos[ahead - LANES][:, lanes].astype(jnp.float32))
            emit(position, taps[-TAPS:])

    pair = 2
    rows_of = lambda place: 2 * freq * place
    count = rows_of(sum(sizes))
    table = table_ref[rows_of(low) : rows_of(low) + count, :]
    for g in range(owned // pair):
        rows = jnp.concatenate(
            [
                jnp.concatenate(
                    [ref[pl.ds(g * pair + u, LANES, stride=owned), :] for ref in (low_ref, high_ref)],
                    axis=1,
                )
                for u in range(pair)
            ],
            axis=0,
        ).astype(jnp.bfloat16)
        result = lax.dot_general(
            table, rows, (((1,), (1,)), ((), ())), preferred_element_type=jnp.float32
        )
        for u in range(pair):
            spec_ref[pl.ds(g * pair + u, count, stride=owned), :] = result[
                :, u * LANES : (u + 1) * LANES
            ]

    channels = CH // freq
    start = 0
    for k, size in enumerate(sizes):
        for u in range(size):
            for dest in range(freq):
                row = (rows_of(start + u) + dest) * owned
                re = spec_ref[row : row + owned, :]
                im = spec_ref[row + freq * owned : row + (freq + 1) * owned, :]
                at = (dest * channels + low + start + u) * owned
                wre, wim = wre_ref[at : at + owned, :], wim_ref[at : at + owned, :]
                outs[k][dest, u, 0] = (wre * re - wim * im).astype(jnp.bfloat16)
                outs[k][dest, u, 1] = (wre * im + wim * re).astype(jnp.bfloat16)
        start += size


def analyse(voltages, window, table, gain_re, gain_im, freq, low, sizes, first, count):
    owned = voltages.shape[0]
    halo = [
        pl.BlockSpec((owned, NFFT), lambda b, q=q: (0, (first + b + 1) * LANES + q))
        for q in range(TAPS - 1)
    ]
    whole = lambda shape: pl.BlockSpec(shape, lambda b: (0, 0))
    return pl.pallas_call(
        functools.partial(analyse_kernel, owned, freq, low, sizes),
        grid=(count,),
        in_specs=[
            pl.BlockSpec((owned, LANES * NFFT), lambda b: (0, first + b)),
            *halo,
            whole((TAPS, NFFT)),
            whole((2 * CH, NFFT)),
            whole((owned, CH)),
            whole((owned, CH)),
        ],
        out_specs=[
            pl.BlockSpec((freq, size, 2, owned, LANES), lambda b: (0, 0, 0, 0, b)) for size in sizes
        ],
        out_shape=[
            jax.ShapeDtypeStruct((freq, size, 2, owned, count * LANES), jnp.bfloat16)
            for size in sizes
        ],
        scratch_shapes=[
            pltpu.VMEM((LANES * owned, LANES), jnp.float32),
            pltpu.VMEM((LANES * owned, LANES), jnp.float32),
            pltpu.VMEM((2 * freq * sum(sizes) * owned, LANES), jnp.float32),
            pltpu.VMEM((CH * owned, LANES), jnp.float32),
            pltpu.VMEM((CH * owned, LANES), jnp.float32),
        ],
        compiler_params=pltpu.CompilerParams(vmem_limit_bytes=VMEM),
        cost_estimate=pl.CostEstimate(
            flops=2 * owned * count * LANES * NFFT * 2 * CH * 8,
            bytes_accessed=4 * owned * count * LANES * NFFT,
            transcendentals=0,
        ),
    )(voltages, voltages, voltages, voltages, window, table, gain_re, gain_im)


def correlate_kernel(steps, me_ref, *rest):
    count = len(steps) + (0 not in steps)
    heads, bodies, out_ref, left_ref = rest[:count], rest[count : 2 * count], rest[-2], rest[-1]
    rows = heads[0].shape[0] * heads[0].shape[3]

    def part(r, p):
        return [ref[r][:, 0, p].reshape(rows, -1) for ref in (heads, bodies)]

    re = jnp.concatenate(part(0, 0), axis=1)
    im = jnp.concatenate(part(0, 1), axis=1)
    left_ref[0:rows, 0:FRAMES] = re
    left_ref[0:rows, FRAMES:] = im
    left_ref[rows:, 0:FRAMES] = im
    left_ref[rows:, FRAMES:] = -re
    factor = 1.0 / FRAMES
    for place, step in enumerate(steps):
        r = count - len(steps) + place
        other = jnp.concatenate([*part(r, 0), *part(r, 1)], axis=1)
        both = lax.dot_general(
            left_ref[...], other, (((1,), (1,)), ((), ())), preferred_element_type=jnp.float32
        )
        column = (me_ref[0] ^ step) % len(steps)
        at = pl.ds(pl.multiple_of(column * rows, rows), rows)
        out_ref[0, 0, :, at] = both[:rows] * factor
        out_ref[1, 0, :, at] = both[rows:] * factor


def correlate(me, tiles, steps, heads, bodies, previous, first, channels):
    freq, size, _, owned, _ = bodies[0].shape
    rows = freq * owned
    width = len(steps)
    in_specs = [
        pl.BlockSpec((freq, 1, 2, owned, x.shape[-1]), lambda c, me: (0, first + c, 0, 0, 0))
        for x in heads
    ] + [
        pl.BlockSpec((freq, 1, 2, owned, x.shape[-1]), lambda c, me: (0, c, 0, 0, 0)) for x in bodies
    ]
    args = [me, *heads, *bodies]
    aliases = {}
    if previous is not None:
        in_specs.append(pl.BlockSpec(memory_space=pl.ANY))
        aliases = {len(args): 0}
        args.append(previous)
    return pl.pallas_call(
        functools.partial(correlate_kernel, steps),
        grid_spec=pltpu.PrefetchScalarGridSpec(
            num_scalar_prefetch=1,
            grid=(size,),
            in_specs=in_specs,
            out_specs=pl.BlockSpec(
                (2, 1, rows, width * rows),
                lambda c, me: (0, first + c, 0, (me[0] ^ steps[0]) // width),
            ),
            scratch_shapes=[pltpu.VMEM((2 * rows, 2 * FRAMES), jnp.bfloat16)],
        ),
        out_shape=jax.ShapeDtypeStruct((2, channels, rows, tiles * rows), jnp.float32),
        input_output_aliases=aliases,
        compiler_params=pltpu.CompilerParams(vmem_limit_bytes=VMEM // 2),
        cost_estimate=pl.CostEstimate(
            flops=size * 2 * (2 * rows) * (2 * FRAMES) * (width * rows),
            bytes_accessed=size * (tiles * rows * FRAMES * 4 + 2 * rows * width * rows * 4),
            transcendentals=0,
        ),
    )(*args)


def per_device(freq, tile, voltages, gain_re, gain_im):
    channels = CH // freq
    sizes = chunk_sizes(channels)
    me = lax.axis_index("tile").astype(jnp.int32).reshape(1)
    tables = (
        window_table(TAPS, NFFT),
        fourier_table(NFFT, CH, FIRST, freq),
        gain_re,
        gain_im,
    )
    blocks = FRAMES // LANES
    messages = list(analyse(voltages, *tables, freq, 0, (channels,), 0, 1))
    lead = len(sizes) // 4
    messages += analyse(voltages, *tables, freq, 0, sizes[:lead], 1, blocks - 1)
    messages[1], again = lax.optimization_barrier((messages[1], voltages))
    messages += analyse(again, *tables, freq, sum(sizes[:lead]), sizes[lead:], 1, blocks - 1)
    if lead > 1:
        messages[lead], messages[lead + 1] = lax.optimization_barrier(
            (messages[lead], messages[lead + 1])
        )

    def swap(array, bit):
        return lax.ppermute(array, "tile", [(t, t ^ bit) for t in range(tile)])

    count = len(messages)
    firsts = [sum(sizes[:k]) for k in range(count)]
    turned, across, beside, opposite, results = ([None] * count for _ in range(5))

    def finish(k, steps):
        parts = (turned, beside, across, opposite)
        wanted = steps if 0 in steps else (0, *steps)
        heads, bodies = ([parts[step][m] for step in wanted] for m in (0, k))
        before = results[k] if results[k] is not None else results[k - 1]
        results[k] = correlate(me, tile, steps, heads, bodies, before, firsts[k - 1], channels)

    def after(array, *waits):
        waits = [w for w in waits if w is not None]
        return lax.optimization_barrier((array, *waits))[0] if waits else array

    lag = 2
    for k in range(count):
        message = messages[k]
        if k >= lag:
            message = after(message, across[k - lag], beside[k - lag])
        if k >= lag + 1:
            message = after(message, opposite[k - lag - 1])
        if k >= lag + 2:
            message = after(message, results[k - lag - 2])
        turned[k] = lax.all_to_all(message, "freq", split_axis=0, concat_axis=0, tiled=True)
        across[k] = swap(turned[k], 2)
        beside[k] = swap(turned[k], 1)
        source = across[k]
        if k == count - 1:
            finish(k, (0, 1))
            source = after(source, results[k])
        opposite[k] = swap(source, 1)
        if k >= 1:
            finish(k, (2, 3) if k == count - 1 else (0, 1, 2, 3))
    return results[-1]


def solution(mesh):
    in_specs = (P(("tile", "freq"), None), P(("tile", "freq"), None), P(("tile", "freq"), None))
    out_specs = P(None, "freq", "tile", None)
    return jax.shard_map(
        functools.partial(per_device, mesh.shape["freq"], mesh.shape["tile"]),
        mesh=mesh,
        in_specs=in_specs,
        out_specs=out_specs,
        check_vma=False,
    )
```
